256 devices in a mesh: blk: 16 (over z, core), grp: 16 (over x, y).
Axes of the slice: x: 4, y: 4, z: 8, core: 2. Of those that a mesh axis runs over, the one named last changes fastest.
Arguments:
- queries: bfloat16 [256, 5120], P(('grp', 'blk')), parts along dimension 0, may hold values from -28 to 28
- cache_keys: bfloat16 [2048, 128, 1024], P(('grp', 'blk')), parts along dimension 0, may hold values from -24 to 24
- pool_values_prior: bfloat16 [2048, 128, 1024], P(('grp', 'blk')), parts along dimension 0, may hold values from -6 to 6
- prefill_keys: bfloat16 [512, 128, 1024], P(('grp', 'blk')), parts along dimension 0, may hold values from -6 to 6
- prefill_values: bfloat16 [512, 128, 1024], P(('grp', 'blk')), parts along dimension 0, may hold values from -6 to 6
- context_lengths: int32 [64], P('grp'), parts along dimension 0, may hold values from 1028 to 4096, as said below
- block_table: int32 [64, 32], P('grp'), parts along dimension 0, may hold values from 0 to 127, as said below
- spill_slots: int32 [512], P('grp'), parts along dimension 0, may hold values from 0 to 127, as said below
Outputs:
- attended: bfloat16 [256, 5120], P(('grp', 'blk')), parts along dimension 0
- pool_keys: bfloat16 [2048, 128, 1024], P(('grp', 'blk')), parts along dimension 0
- pool_values: bfloat16 [2048, 128, 1024], P(('grp', 'blk')), parts along dimension 0
The draws below stay inside these ranges and needn't reach their ends.
There are 16 independent parts, one for each index of `grp`. The reference program is written for one: setup_inputs(seed, part) draws one part's arguments, and reference() takes and returns one part's arrays. A program takes and returns all parts, laid end to end along the dimension named above; each array names one. Nothing has to cross between parts.
Inputs may be any that keep to these rules, and one draw needn't show every extreme that they name: Every pool block appears exactly once in block_table, so each request owns 32 blocks. `spill_slots`: distinct pool blocks; exactly 2 of them lie in each rank's range of 8 blocks, and each stands among the first 8 columns of some row of block_table. `context_lengths`: some request has 4096 tokens.
All inputs are finite; a program needn't handle non-finite values.
Results may differ from the reference program's by a relative error of at most 0.0045.
Values may be sent and summed in bfloat16 or wider, within the bound.
No kernel may reach another device: no remote copies, remote signals or barrier semaphores. Data moves between devices by JAX's collectives and lax.ppermute only.
A program may use at most 128 MiB of HBM per device.

```python
import jax
import jax.numpy as jnp
from jax import lax

QUERY_HEADS = 40
KEY_VALUE_HEADS = 8
HEAD_SIZE = 128
BLOCK_TOKENS = 128
STEPS = 4
REQ = 4
PF_DEV = 2
RANK_BLOCKS = 8
POOL_BLOCKS = 128
MAXB = 32
QUERY_ROWS = 16
PREFILL_BLOCKS = 32
N_BLK = 16


def placement(key):
    ranks = POOL_BLOCKS // RANK_BLOCKS
    rank_keys = jax.random.split(jax.random.fold_in(key, 101), ranks)
    within = jax.vmap(lambda single: jax.random.permutation(single, RANK_BLOCKS))(rank_keys).astype(jnp.int32)
    base = (jnp.arange(ranks, dtype=jnp.int32) * RANK_BLOCKS)[:, None]
    chosen = (base + within[:, :PF_DEV]).reshape(-1)
    others = (base + within[:, PF_DEV:]).reshape(-1)
    chosen = jax.random.permutation(jax.random.fold_in(key, 102), chosen).astype(jnp.int32)
    others = jax.random.permutation(jax.random.fold_in(key, 103), others).astype(jnp.int32)
    leading = PREFILL_BLOCKS // REQ
    table = jnp.concatenate([chosen.reshape(REQ, leading), others.reshape(REQ, MAXB - leading)], axis=1)
    return (table.astype(jnp.int32), chosen)


def draw_block_table(key, part):
    table, chosen = placement(key)
    return table


def draw_spill_slots(key, part):
    table, chosen = placement(key)
    return chosen


def draw_context_lengths(key, part):
    key = jax.random.fold_in(key, 5)
    first_block, second = jax.random.split(key)
    lengths = jax.random.randint(first_block, (REQ,), PREFILL_BLOCKS // REQ * BLOCK_TOKENS + STEPS, MAXB * BLOCK_TOKENS + 1)
    longest = jax.random.randint(second, (), 0, REQ)
    return jnp.where(jnp.arange(REQ) == longest, MAXB * BLOCK_TOKENS, lengths).astype(jnp.int32)


def draw_cache_keys(key, part):
    key = jax.random.fold_in(key, 7)
    first_block = jax.random.fold_in(key, 0)
    random_offset = jnp.clip(jax.random.normal(first_block, (POOL_BLOCKS, BLOCK_TOKENS, KEY_VALUE_HEADS * HEAD_SIZE), jnp.float32), -3.5, 3.5)
    return random_offset.astype(jnp.bfloat16)


def draw_queries(key, part):
    key = jax.random.fold_in(key, 9)
    first_block = jax.random.fold_in(key, 0)
    random_offset = jnp.clip(jax.random.normal(first_block, (QUERY_ROWS, QUERY_HEADS * HEAD_SIZE), jnp.float32), -3.5, 3.5)
    return random_offset.astype(jnp.bfloat16)


def level_of(own_key, shape, cuts, least, high):
    loudness, own = 1.0, jax.random.fold_in(own_key, 6)
    for axis_at, shards_of in cuts:
        steps = jnp.exp(jax.random.uniform(jax.random.fold_in(own, axis_at), (shards_of,), jnp.float32, least / len(cuts), high / len(cuts)))
        loudness = loudness * jnp.repeat(steps, shape[axis_at] // shards_of).reshape([-1 if axis == axis_at else 1 for axis in range(len(shape))])
    return loudness


def scatter_about(rng, dims, scale, most, cuts=(), kind=jnp.bfloat16):
    values = scale * jax.random.normal(rng, dims, jnp.float32)
    if cuts:
        values = values * level_of(rng, dims, cuts, -0.22, 0.18)
    return jnp.clip(values, -most, most).astype(kind)


def setup_inputs(seed: int = 0, part: int = 0) -> dict:
    keys = jax.random.split(jax.random.key(seed), 9)
    part_splits = jax.random.split(jax.random.fold_in(keys[8], part), 9)
    queries = draw_queries(jax.random.fold_in(jax.random.fold_in(keys[8], part), 71), part)
    cache_keys = draw_cache_keys(jax.random.fold_in(jax.random.fold_in(keys[8], part), 71), part)
    pool_values_prior = scatter_about(part_splits[2], (POOL_BLOCKS, BLOCK_TOKENS, KEY_VALUE_HEADS * HEAD_SIZE), 1.0, 6.0, ((0, 16),))
    prefill_keys = scatter_about(part_splits[3], (PREFILL_BLOCKS, BLOCK_TOKENS, KEY_VALUE_HEADS * HEAD_SIZE), 1.0, 6.0, ((0, 16),))
    prefill_values = scatter_about(part_splits[4], (PREFILL_BLOCKS, BLOCK_TOKENS, KEY_VALUE_HEADS * HEAD_SIZE), 1.0, 6.0, ((0, 16),))
    context_lengths = draw_context_lengths(jax.random.fold_in(jax.random.fold_in(keys[8], part), 71), part)
    block_table = draw_block_table(jax.random.fold_in(jax.random.fold_in(keys[8], part), 71), part)
    spill_slots = draw_spill_slots(jax.random.fold_in(jax.random.fold_in(keys[8], part), 71), part)
    return {"queries": queries, "cache_keys": cache_keys, "pool_values_prior": pool_values_prior, "prefill_keys": prefill_keys, "prefill_values": prefill_values, "context_lengths": context_lengths, "block_table": block_table, "spill_slots": spill_slots}


NEGATIVE_LARGE = -1.0e30


def merge_state(running, incoming):
    run_max, run_sum, run_out = running
    new_max, new_sum, new_out = incoming
    largest = jnp.maximum(run_max, new_max)
    keep = jnp.exp(run_max - largest)
    take = jnp.exp(new_max - largest)
    return (largest, run_sum * keep + new_sum * take, run_out * keep[..., None] + new_out * take[..., None])


def rank_partial(queries, keys_of_block, values_of_block, owner, limit):
    head_groups = QUERY_HEADS // KEY_VALUE_HEADS
    row_ids = jnp.arange(QUERY_ROWS, dtype=jnp.int32)
    step_of = row_ids // REQ
    request_of = row_ids % REQ
    query_head_rows = queries.astype(jnp.float32).reshape(QUERY_ROWS, KEY_VALUE_HEADS, head_groups, HEAD_SIZE)
    key_head_rows = keys_of_block.astype(jnp.float32).reshape(RANK_BLOCKS, BLOCK_TOKENS, KEY_VALUE_HEADS, HEAD_SIZE)
    scores = jnp.einsum("rhgd,sthd->rhgst", query_head_rows, key_head_rows, precision=lax.Precision.HIGHEST) * (HEAD_SIZE ** -0.5)
    bound = limit[None, :] - (STEPS - 1) + step_of[:, None]
    visible = jnp.arange(BLOCK_TOKENS, dtype=jnp.int32)[None, None, :] < bound[:, :, None]
    visible = visible & (owner[None, :] == request_of[:, None])[:, :, None]
    visible = visible[:, None, None]
    masked = jnp.where(visible, scores, NEGATIVE_LARGE)
    row_max = jnp.max(masked, axis=(-2, -1))
    weights = jnp.where(visible, jnp.exp(masked - row_max[..., None, None]), jnp.float32(0.0))
    row_sum = jnp.sum(weights, axis=(-2, -1))
    probs = weights.astype(jnp.bfloat16).astype(jnp.float32)
    value_head_rows = values_of_block.astype(jnp.float32).reshape(RANK_BLOCKS, BLOCK_TOKENS, KEY_VALUE_HEADS, HEAD_SIZE)
    row_out = jnp.einsum("rhgst,sthd->rhgd", probs, value_head_rows, precision=lax.Precision.HIGHEST)
    return (row_max, row_sum, row_out)


def reference(queries, cache_keys, pool_values_prior, prefill_keys, prefill_values, context_lengths, block_table, spill_slots):
    pool_keys = cache_keys.at[spill_slots].set(prefill_keys)
    pool_values = pool_values_prior.at[spill_slots].set(prefill_values)
    blocks = jnp.arange(POOL_BLOCKS, dtype=jnp.int32)
    match = block_table[:, :, None] == blocks[None, None, :]
    request_ids = jnp.arange(REQ, dtype=jnp.int32)[:, None, None]
    owner = jnp.sum(jnp.where(match, request_ids, 0), axis=(0, 1)).astype(jnp.int32)
    column = jnp.arange(MAXB, dtype=jnp.int32)[None, :, None]
    limit = jnp.sum(jnp.where(match, context_lengths[:, None, None] - column * BLOCK_TOKENS, 0), axis=(0, 1)).astype(jnp.int32)
    head_groups = QUERY_HEADS // KEY_VALUE_HEADS
    start_offset = (jnp.full((QUERY_ROWS, KEY_VALUE_HEADS, head_groups), NEGATIVE_LARGE, jnp.float32),
             jnp.zeros((QUERY_ROWS, KEY_VALUE_HEADS, head_groups), jnp.float32),
             jnp.zeros((QUERY_ROWS, KEY_VALUE_HEADS, head_groups, HEAD_SIZE), jnp.float32))

    def visit(running, rank):
        first_block = (rank * RANK_BLOCKS).astype(jnp.int32)
        keys_of_block = lax.dynamic_slice_in_dim(pool_keys, first_block, RANK_BLOCKS, 0)
        values_of_block = lax.dynamic_slice_in_dim(pool_values, first_block, RANK_BLOCKS, 0)
        block_owner = lax.dynamic_slice_in_dim(owner, first_block, RANK_BLOCKS, 0)
        block_limit = lax.dynamic_slice_in_dim(limit, first_block, RANK_BLOCKS, 0)
        partial_state = rank_partial(queries, keys_of_block, values_of_block, block_owner, block_limit)
        return merge_state(running, partial_state), None

    final, unused = lax.scan(visit, start_offset, jnp.arange(N_BLK, dtype=jnp.int32))
    attended = final[2] / final[1][..., None]
    attended = attended.reshape(QUERY_ROWS, QUERY_HEADS * HEAD_SIZE).astype(jnp.bfloat16)
    return (attended, pool_keys, pool_values)
```

```python
import jax
import jax.numpy as jnp
from jax import lax
from jax.experimental import pallas as pl
from jax.experimental.pallas import tpu as pltpu
from jax.sharding import PartitionSpec as P

RANKS = 16
SLOTS = 8
SPILL = 32
REQ = 4
STEPS = 4
COLS = 32
TOK = 128
HEADS = 8
GROUP = 5
DIM = 128
WIDTH = HEADS * DIM
HALF = 64
DATA = 256
TAIL = 48
NEG = -1e30
ANY = pl.BlockSpec(memory_space=pl.ANY)
SMEM = pl.BlockSpec(memory_space=pltpu.SMEM)
VMEM = pl.BlockSpec(memory_space=pltpu.VMEM)
F32 = jnp.float32
BF16 = jnp.bfloat16


def attend_kernel(
    spill, table, lengths, q_ref, ck, cv, pk, pv,
    out_k, out_v, tail_ref,
    inverse, taken, slot_of, kbuf, vbuf, m_s, l_s, o_s, row_s, in_sem, out_sem,
):
    me = lax.axis_index("blk")
    own = SLOTS - 2

    def pre(i):
        return (
            pltpu.make_async_copy(pk.at[i], kbuf.at[own + i], in_sem.at[0, own + i]),
            pltpu.make_async_copy(pv.at[i], vbuf.at[own + i], in_sem.at[1, own + i]),
        )

    def read(e):
        s = slot_of[e]
        return (
            pltpu.make_async_copy(ck.at[s], kbuf.at[e], in_sem.at[0, e]),
            pltpu.make_async_copy(cv.at[s], vbuf.at[e], in_sem.at[1, e]),
        )

    def write(e):
        s = slot_of[e]
        return (
            pltpu.make_async_copy(kbuf.at[e], out_k.at[s], out_sem.at[0, e]),
            pltpu.make_async_copy(vbuf.at[e], out_v.at[s], out_sem.at[1, e]),
        )

    for i in range(2):
        for c in pre(i):
            c.start()
    for s in range(SLOTS):
        taken[s] = 0

    def mark(b, _):
        t = spill[b]

        @pl.when((t >> 3) == me)
        def _():
            taken[t & 7] = 1

        return 0

    lax.fori_loop(0, SPILL, mark, 0)

    def pick(s, n):
        @pl.when(taken[s] == 0)
        def _():
            slot_of[n] = s

        return n + 1 - taken[s]

    lax.fori_loop(0, SLOTS, pick, 0)
    for e in range(own):
        for c in read(e):
            c.start()

    def invert(i, _):
        for r in range(REQ):
            inverse[table[r, i]] = r * COLS + i
        return 0

    lax.fori_loop(0, COLS, invert, 0)
    m_s[...] = jnp.full_like(m_s, NEG)
    l_s[...] = jnp.zeros_like(l_s)
    o_s[...] = jnp.zeros_like(o_s)
    rows = HEADS * 32
    step = (lax.broadcasted_iota(jnp.int32, (rows, TOK), 0) & 31) >> 3
    token = lax.broadcasted_iota(jnp.int32, (rows, TOK), 1) - step

    def visit(e, block):
        place = inverse[block]
        r = place >> 5
        bound = lengths[r] - (place & 31) * TOK - (STEPS - 1)
        visible = token < bound
        s = jnp.concatenate(
            [
                lax.dot_general(
                    q_ref[r, h], kbuf[e, :, h * DIM : (h + 1) * DIM],
                    (((1,), (1,)), ((), ())), preferred_element_type=F32,
                )
                for h in range(HEADS)
            ],
            axis=0,
        ) * (DIM ** -0.5)
        s = jnp.where(visible, s, NEG)
        top = jnp.broadcast_to(jnp.max(s, axis=1, keepdims=True), (rows, TOK))
        old = m_s[r]
        new = jnp.maximum(old, top)
        keep = jnp.exp(old - new)
        w = jnp.where(visible, jnp.exp(s - new), 0.0)
        m_s[r] = new
        l_s[r] = l_s[r] * keep + jnp.sum(w, axis=1, keepdims=True)
        p = w.astype(BF16)
        o = jnp.concatenate(
            [
                jnp.dot(
                    p[h * 32 : (h + 1) * 32], vbuf[e, :, h * DIM : (h + 1) * DIM],
                    preferred_element_type=F32,
                )
                for h in range(HEADS)
            ],
            axis=0,
        )
        o_s[r] = o_s[r] * keep + o

    for i in range(2):
        for c in pre(i):
            c.wait()

    def fresh(i, _):
        visit(own + i, spill[me * 2 + i])
        return 0

    lax.fori_loop(0, 2, fresh, 0)

    def stay(e, _):
        for c in read(e):
            c.wait()
        for c in write(e):
            c.start()
        visit(e, me * SLOTS + slot_of[e])
        return 0

    lax.fori_loop(0, own, stay, 0)

    sub = lax.broadcasted_iota(jnp.int32, (8, DIM), 0)
    lane = lax.broadcasted_iota(jnp.int32, (8, DIM), 1)

    def pack(r, _):
        for a in range(STEPS):
            for h in range(HEADS):
                at = h * 32 + a * 8
                m = m_s[r, at : at + 8, :]
                l = l_s[r, at : at + 8, :]
                hi = l.astype(BF16).astype(F32)
                lo = l - hi
                m_hi = m.astype(BF16).astype(F32)
                m_mid = (m - m_hi).astype(BF16).astype(F32)
                m_lo = m - m_hi - m_mid
                ml = jnp.zeros((8, DIM), F32)
                for n, term in enumerate((m_hi, m_mid, m_lo, hi, lo)):
                    ml = jnp.where(lane == sub + 8 * n, term, ml)
                ml = jnp.sum(ml, axis=0, keepdims=True)
                o = o_s[r, at : at + 8, :]
                row_s[h * 6 : h * 6 + 6, :] = jnp.where(sub == GROUP, ml, o)[:6]
            tail_ref[a * REQ + r] = row_s[...].astype(BF16)
        return 0

    lax.fori_loop(0, REQ, pack, 0)
    for e in range(own):
        for c in write(e):
            c.wait()


def sort_kernel(spill, y, tail, out, count, sem, tail_sem):
    copy = pltpu.make_async_copy(tail, out.at[:, pl.ds(DATA, TAIL)], tail_sem)
    copy.start()
    for k in range(RANKS):
        count[k] = 0

    def send(b, _):
        t = spill[b] >> 3
        n = count[t]
        count[t] = n + 1
        pltpu.make_async_copy(
            y.at[b >> 1, pl.ds(pl.multiple_of((b & 1) * 128, 128), 128)],
            out.at[t, pl.ds(pl.multiple_of(n * 128, 128), 128)],
            sem,
        ).start()
        return 0

    lax.fori_loop(0, SPILL, send, 0)
    pltpu.make_async_copy(y, out.at[:, pl.ds(0, DATA)], sem).wait()
    copy.wait()


def place_kernel(spill, z, key_in, value_in, att, out_k, out_v, slot_of, tail, sem, tail_sem):
    me = lax.axis_index("blk")
    copy = pltpu.make_async_copy(z.at[:, pl.ds(DATA, TAIL)], tail, tail_sem)
    copy.start()

    def find(b, n):
        t = spill[b]
        mine = (t >> 3) == me

        @pl.when(mine)
        def _():
            slot_of[n] = t & 7

        return n + jnp.where(mine, 1, 0)

    lax.fori_loop(0, SPILL, find, 0)
    for q in range(2):
        s = slot_of[q]
        for c in range(RANKS):
            for kv, out in enumerate((out_k, out_v)):
                pltpu.make_async_copy(
                    z.at[c, pl.ds(q * 128 + kv * HALF, HALF)],
                    out.at[s, pl.ds((c % 2) * HALF, HALF), pl.ds((c // 2) * DIM, DIM)],
                    sem,
                ).start()
    copy.wait()
    sub = lax.broadcasted_iota(jnp.int32, (8, DIM), 0)
    lane = lax.broadcasted_iota(jnp.int32, (8, DIM), 1)
    for h in range(HEADS):
        part = [tail[k, h * 6 : h * 6 + 6, :].astype(F32) for k in range(RANKS)]
        ml = jnp.concatenate([x[5:6] for x in part], axis=0)
        peak = ml + (pltpu.roll(ml, DIM - 8, 1) + pltpu.roll(ml, DIM - 16, 1))
        scale = jnp.exp(peak - jnp.max(peak, axis=0, keepdims=True))
        total = pltpu.roll(ml, DIM - 24, 1) + pltpu.roll(ml, DIM - 32, 1)
        down = jnp.sum(scale * total, axis=0, keepdims=True)
        scale = jnp.where(lane[:1] < 8, scale / down, 0.0)
        acc = jnp.zeros((6, DIM), F32)
        for k in range(RANKS):
            col = jnp.sum(jnp.where(lane[:6] == sub[:6], scale[k : k + 1], 0.0), axis=1, keepdims=True)
            acc = acc + col * part[k]
        for g in range(GROUP):
            n = h * GROUP + g
            att[:, n * DIM : (n + 1) * DIM] = acc[g : g + 1].astype(BF16)
    pltpu.make_async_copy(z.at[:, pl.ds(0, DATA)], z.at[:, pl.ds(0, DATA)], sem).wait()


def per_device(queries, cache_keys, values_prior, prefill_keys, prefill_values, lengths, table, spill):
    gathered = lax.all_gather(queries, "blk", axis=0, tiled=True)
    packed = jnp.stack([prefill_keys, prefill_values], axis=1)
    packed = packed.reshape(2, 2, 2, HALF, HEADS, DIM).transpose(4, 2, 0, 1, 3, 5)
    packed = packed.reshape(RANKS, DATA, DIM)
    spread = lax.all_to_all(packed, "blk", split_axis=0, concat_axis=0, tiled=True)

    q = gathered.reshape(STEPS, REQ, HEADS, GROUP, DIM).transpose(1, 2, 0, 3, 4)
    q = jnp.pad(q, ((0, 0), (0, 0), (0, 0), (0, 8 - GROUP), (0, 0))).reshape(REQ, HEADS, 32, DIM)
    pool = jax.ShapeDtypeStruct(cache_keys.shape, BF16)
    rows = HEADS * 32
    keys, values, tail = pl.pallas_call(
        attend_kernel,
        out_shape=(pool, pool, jax.ShapeDtypeStruct((RANKS, TAIL, DIM), BF16)),
        in_specs=[SMEM, SMEM, SMEM, VMEM, ANY, ANY, ANY, ANY],
        out_specs=(ANY, ANY, VMEM),
        scratch_shapes=[
            pltpu.SMEM((RANKS * SLOTS,), jnp.int32),
            pltpu.SMEM((SLOTS,), jnp.int32),
            pltpu.SMEM((SLOTS,), jnp.int32),
            pltpu.VMEM((SLOTS, TOK, WIDTH), BF16),
            pltpu.VMEM((SLOTS, TOK, WIDTH), BF16),
            pltpu.VMEM((REQ, rows, DIM), F32),
            pltpu.VMEM((REQ, rows, DIM), F32),
            pltpu.VMEM((REQ, rows, DIM), F32),
            pltpu.VMEM((TAIL, DIM), F32),
            pltpu.SemaphoreType.DMA((2, SLOTS)),
            pltpu.SemaphoreType.DMA((2, SLOTS)),
        ],
        compiler_params=pltpu.CompilerParams(vmem_limit_bytes=32 << 20),
        cost_estimate=pl.CostEstimate(flops=2 ** 30, bytes_accessed=2 ** 24, transcendentals=2 ** 20),
        name="attend",
    )(spill, table, lengths, q, cache_keys, values_prior, prefill_keys, prefill_values)

    sent = pl.pallas_call(
        sort_kernel,
        out_shape=jax.ShapeDtypeStruct((RANKS, DATA + TAIL, DIM), BF16),
        in_specs=[SMEM, VMEM, VMEM],
        out_specs=ANY,
        scratch_shapes=[pltpu.SMEM((RANKS,), jnp.int32), pltpu.SemaphoreType.DMA, pltpu.SemaphoreType.DMA],
        name="sort",
    )(spill, spread, tail)
    landed = lax.all_to_all(sent, "blk", split_axis=0, concat_axis=0, tiled=True)

    return pl.pallas_call(
        place_kernel,
        out_shape=(jax.ShapeDtypeStruct(queries.shape, BF16), pool, pool),
        in_specs=[SMEM, ANY, ANY, ANY],
        out_specs=(VMEM, ANY, ANY),
        scratch_shapes=[
            pltpu.SMEM((SLOTS,), jnp.int32),
            pltpu.VMEM((RANKS, TAIL, DIM), BF16),
            pltpu.SemaphoreType.DMA,
            pltpu.SemaphoreType.DMA,
        ],
        input_output_aliases={2: 1, 3: 2},
        compiler_params=pltpu.CompilerParams(vmem_limit_bytes=16 << 20),
        name="place",
    )(spill, landed, keys, values)


def solution(mesh):
    both = ("grp", "blk")
    return jax.shard_map(
        per_device,
        mesh=mesh,
        in_specs=(P(both, None), *[P(both, None, None)] * 4, P("grp"), P("grp", None), P("grp")),
        out_specs=(P(both, None), P(both, None, None), P(both, None, None)),
        check_vma=False,
    )
```

```python
import jax
import jax.numpy as jnp
from jax import lax
from jax.experimental import pallas as pl
from jax.experimental.pallas import tpu as pltpu
from jax.sharding import PartitionSpec as P

RANKS = 16
SLOTS = 8
KEPT = 6
SPILL = 32
REQ = 4
STEPS = 4
COLS = 32
TOK = 128
HEADS = 8
GROUP = 5
DIM = 128
WIDTH = HEADS * DIM
HALF = 64
DATA = 256
TAIL = 48
LENGTHS = 32
TABLE = 64
REQUEST = 32
BOUND = 40
HOME = 48
PLAN = 64
NEG = -1e30
ANY = pl.BlockSpec(memory_space=pl.ANY)
SMEM = pl.BlockSpec(memory_space=pltpu.SMEM)
VMEM = pl.BlockSpec(memory_space=pltpu.VMEM)
HBM = pl.BlockSpec(memory_space=pltpu.HBM)
DMA = pltpu.SemaphoreType.DMA
F32 = jnp.float32
BF16 = jnp.bfloat16


def pack_kernel(q, pk, pv, out, q_in, q_rows, buf, q_sem, sem):
    get = pltpu.make_async_copy(q, q_in, q_sem)
    get.start()
    loads = []
    for b in range(2):
        for kv, source in enumerate((pk, pv)):
            for half in range(2):
                n = b * 4 + kv * 2 + half
                loads.append(pltpu.make_async_copy(source.at[b, pl.ds(half * HALF, HALF)], buf.at[n], sem.at[n]))
                loads[-1].start()
    q_rows[...] = jnp.zeros_like(q_rows)
    get.wait()
    for n in range(HEADS * GROUP):
        q_rows[n : n + 1, :] = q_in[:, n * DIM : (n + 1) * DIM].astype(F32)
    q_bf = q_rows[...].astype(BF16)
    for k in range(RANKS):
        out[k, DATA:, :] = q_bf
    for n, load in enumerate(loads):
        load.wait()
        at = (n >> 1) * HALF
        for h in range(HEADS):
            out[2 * h + (n & 1), at : at + HALF, :] = buf[n, :, h * DIM : (h + 1) * DIM]


def load_kernel(
    ints, ck, cv, pk, pv, out_k, out_v, reads_out, plan,
    inverse, taken, slot_of, count, buf, in_sem, out_sem, get_sem,
):
    me = lax.axis_index("blk")
    reads, writes = [], []
    for i in range(2):
        for kv, source in enumerate((pk, pv)):
            e = KEPT + i
            reads.append(pltpu.make_async_copy(source.at[i], buf.at[kv, e], in_sem.at[kv, e]))
            writes.append([pltpu.make_async_copy(buf.at[kv, e], reads_out.at[kv, e], get_sem.at[kv, e])])
            reads[-1].start()
    for s in range(SLOTS):
        taken[s] = 0
    for k in range(RANKS):
        count[k] = 0
    for k in range(PLAN):
        plan[k] = 0

    def mark(b, _):
        slot = ints[b]
        t = slot >> 3
        n = count[t]
        count[t] = n + 1
        plan[b] = t * 2 + n

        @pl.when(t == me)
        def _():
            taken[slot & 7] = 1
            plan[HOME + n] = slot & 7

        return 0

    lax.fori_loop(0, SPILL, mark, 0)

    def pick(s, n):
        @pl.when(taken[s] == 0)
        def _():
            slot_of[n] = s

        return n + 1 - taken[s]

    lax.fori_loop(0, SLOTS, pick, 0)
    for e in range(KEPT):
        s = slot_of[e]
        for kv, (source, out) in enumerate(((ck, out_k), (cv, out_v))):
            reads.append(pltpu.make_async_copy(source.at[s], buf.at[kv, e], in_sem.at[kv, e]))
            writes.append([
                pltpu.make_async_copy(buf.at[kv, e], reads_out.at[kv, e], get_sem.at[kv, e]),
                pltpu.make_async_copy(buf.at[kv, e], out.at[s], out_sem.at[kv, e]),
            ])
            reads[-1].start()

    def invert(i, _):
        for r in range(REQ):
            inverse[ints[TABLE + r * COLS + i]] = r * COLS + i
        return 0

    lax.fori_loop(0, COLS, invert, 0)
    for e in range(SLOTS):
        place = inverse[me * SLOTS + slot_of[e] if e < KEPT else ints[me * 2 + (e - KEPT)]]
        plan[REQUEST + e] = place >> 5
        plan[BOUND + e] = ints[LENGTHS + (place >> 5)] - (place & 31) * TOK - (STEPS - 1)
    for r, w in zip(reads, writes):
        r.wait()
        for c in w:
            c.start()
    for w in writes:
        for c in w:
            c.wait()


def attend_kernel(
    plan, spread, blocks, sent, kbuf, vbuf, q_rows, q_s, s_buf, top_s, m_s, l_s, o_s, row_s, sem
):
    order = tuple(range(SLOTS))
    loads = {}
    for e in order:
        for kv, buf in enumerate((kbuf, vbuf)):
            loads[e, kv] = pltpu.make_async_copy(blocks.at[kv, e], buf.at[e], sem.at[kv, e])
    for kv in range(2):
        for e in order:
            loads[e, kv].start()
    m_s[...] = jnp.full_like(m_s, NEG)
    l_s[...] = jnp.zeros_like(l_s)
    o_s[...] = jnp.zeros_like(o_s)
    q_s[...] = jnp.zeros_like(q_s)
    request = [plan[REQUEST + e] for e in range(SLOTS)]
    bound = [plan[BOUND + e] for e in range(SLOTS)]
    for i in range(RANKS):
        a, r = i // REQ, i % REQ
        q_rows[i] = spread[i, DATA:, :].astype(F32)
        for h in range(HEADS):
            q_s[r, h, a * 8 : a * 8 + GROUP, :] = q_rows[i, h * GROUP : (h + 1) * GROUP, :]
    rows = HEADS * 32
    step = (lax.broadcasted_iota(jnp.int32, (rows, TOK), 0) & 31) >> 3
    token = lax.broadcasted_iota(jnp.int32, (rows, TOK), 1) - step
    for n, e in enumerate(order):
        if n % 2 == 0:
            loads[order[n], 0].wait()
            loads[order[n + 1], 0].wait()
        s = jnp.concatenate(
            [
                lax.dot_general(
                    q_s[request[e], h].astype(BF16), kbuf[e, :, h * DIM : (h + 1) * DIM],
                    (((1,), (1,)), ((), ())), preferred_element_type=F32,
                )
                for h in range(HEADS)
            ],
            axis=0,
        ) * (DIM ** -0.5)
        s = jnp.where(token < bound[e], s, NEG)
        s_buf[e] = s
        top_s[e] = jnp.broadcast_to(jnp.max(s, axis=1, keepdims=True), (rows, TOK))
    for b in range(SPILL):
        to = plan[b]
        sent[to >> 1, pl.ds(pl.multiple_of((to & 1) * 128, 128), 128), :] = spread[
            b >> 1, (b & 1) * 128 : (b & 1) * 128 + 128, :
        ]
    for e in range(SLOTS):
        m_s[request[e]] = jnp.maximum(m_s[request[e]], top_s[e])
    for n, e in enumerate(order):
        if n % 4 == 0:
            for other in order[n : n + 4]:
                loads[other, 1].wait()
        w = jnp.where(token < bound[e], jnp.exp(s_buf[e] - m_s[request[e]]), 0.0)
        p = w.astype(BF16)
        o = jnp.concatenate(
            [
                jnp.dot(
                    p[h * 32 : (h + 1) * 32], vbuf[e, :, h * DIM : (h + 1) * DIM],
                    preferred_element_type=F32,
                )
                for h in range(HEADS)
            ],
            axis=0,
        )
        top_s[e] = jnp.broadcast_to(jnp.sum(w, axis=1, keepdims=True), (rows, TOK))
        s_buf[e] = o
    for e in range(SLOTS):
        l_s[request[e]] = l_s[request[e]] + top_s[e]
        o_s[request[e]] = o_s[request[e]] + s_buf[e]

    sub = lax.broadcasted_iota(jnp.int32, (8, DIM), 0)
    lane = lax.broadcasted_iota(jnp.int32, (8, DIM), 1)
    for r in range(REQ):
        for a in range(STEPS):
            for h in range(HEADS):
                at = h * 32 + a * 8
                row_s[r, a, h * GROUP : (h + 1) * GROUP, :] = o_s[r, at : at + GROUP, :]
                ml = jnp.where(lane == sub, m_s[r, at : at + 8, :], 0.0)
                ml = jnp.where(lane == sub + 8, l_s[r, at : at + 8, :], ml)
                row_s[r, a, 40 + h : 41 + h, :] = jnp.sum(ml, axis=0, keepdims=True)
            ml = row_s[r, a, 40:, :]
            hi = ml.astype(BF16).astype(F32)
            mid = (ml - hi).astype(BF16).astype(F32)
            row_s[r, a, 40:, :] = hi + pltpu.roll(mid, 16, 1) + pltpu.roll(ml - hi - mid, 32, 1)
            sent[a * REQ + r, DATA:, :] = row_s[r, a].astype(BF16)


def place_kernel(plan, z, key_in, value_in, att, out_k, out_v, tail, sem):
    for n in range(2):
        slot = plan[HOME + n]
        for c in range(RANKS):
            for kv, out in enumerate((out_k, out_v)):
                pltpu.make_async_copy(
                    z.at[c, pl.ds(n * 128 + kv * HALF, HALF)],
                    out.at[slot, pl.ds((c % 2) * HALF, HALF), pl.ds((c // 2) * DIM, DIM)],
                    sem,
                ).start()
    for k in range(RANKS):
        tail[k] = z[k, DATA:, :].astype(F32)
    sub = lax.broadcasted_iota(jnp.int32, (8, DIM), 0)
    lane = lax.broadcasted_iota(jnp.int32, (8, DIM), 1)
    state = []
    for k in range(RANKS):
        ml = tail[k, 40:, :]
        state.append(ml + (pltpu.roll(ml, DIM - 16, 1) + pltpu.roll(ml, DIM - 32, 1)))
    top = state[0]
    for x in state[1:]:
        top = jnp.maximum(top, x)
    scales = [jnp.exp(x - top) for x in state]
    down = jnp.zeros((8, DIM), F32)
    for x, scale in zip(state, scales):
        down = down + scale * pltpu.roll(x, DIM - 8, 1)
    inverse = jnp.where(lane < GROUP, 1.0 / jnp.where(lane < GROUP, down, 1.0), 0.0)
    scales = [jnp.where(lane < GROUP, scale, 0.0) * inverse for scale in scales]
    for h in range(HEADS):
        acc = jnp.zeros((GROUP, DIM), F32)
        for k in range(RANKS):
            col = jnp.sum(jnp.where(lane == sub, scales[k][h : h + 1], 0.0), axis=1, keepdims=True)
            acc = acc + col[:GROUP] * tail[k, h * GROUP : (h + 1) * GROUP, :]
        for g in range(GROUP):
            n = h * GROUP + g
            att[:, n * DIM : (n + 1) * DIM] = acc[g : g + 1].astype(BF16)
    pltpu.make_async_copy(z.at[:, pl.ds(0, DATA)], z.at[:, pl.ds(0, DATA)], sem).wait()


def per_device(queries, cache_keys, values_prior, prefill_keys, prefill_values, lengths, table, spill):
    pool = jax.ShapeDtypeStruct(cache_keys.shape, BF16)
    message = jax.ShapeDtypeStruct((RANKS, DATA + TAIL, DIM), BF16)
    rows = HEADS * 32
    ints = jnp.concatenate([spill, lengths, jnp.zeros((TABLE - LENGTHS - REQ,), jnp.int32), table.reshape(-1)])
    packed = pl.pallas_call(
        pack_kernel,
        out_shape=message,
        in_specs=[HBM] * 3,
        out_specs=VMEM,
        scratch_shapes=[
            pltpu.VMEM(queries.shape, BF16),
            pltpu.VMEM((TAIL, DIM), F32),
            pltpu.VMEM((8, HALF, WIDTH), BF16),
            DMA,
            DMA((8,)),
        ],
        compiler_params=pltpu.CompilerParams(vmem_limit_bytes=59 << 20),
        name="pack",
    )(queries, prefill_keys, prefill_values)
    spread = lax.all_to_all(packed, "blk", split_axis=0, concat_axis=0, tiled=True)

    keys, values, blocks, plan = pl.pallas_call(
        load_kernel,
        out_shape=(
            pool,
            pool,
            jax.ShapeDtypeStruct((2, SLOTS, TOK, WIDTH), BF16),
            jax.ShapeDtypeStruct((PLAN,), jnp.int32),
        ),
        in_specs=[SMEM] + [HBM] * 4,
        out_specs=(HBM, HBM, HBM, SMEM),
        scratch_shapes=[
            pltpu.SMEM((RANKS * SLOTS,), jnp.int32),
            pltpu.SMEM((SLOTS,), jnp.int32),
            pltpu.SMEM((SLOTS,), jnp.int32),
            pltpu.SMEM((RANKS,), jnp.int32),
            pltpu.VMEM((2, SLOTS, TOK, WIDTH), BF16),
            DMA((2, SLOTS)),
            DMA((2, SLOTS)),
            DMA((2, SLOTS)),
        ],
        compiler_params=pltpu.CompilerParams(vmem_limit_bytes=58 << 20),
        cost_estimate=pl.CostEstimate(flops=0, bytes_accessed=7 << 20, transcendentals=0),
        name="load",
    )(ints, cache_keys, values_prior, prefill_keys, prefill_values)

    sent = pl.pallas_call(
        attend_kernel,
        out_shape=message,
        in_specs=[SMEM, VMEM, HBM],
        out_specs=VMEM,
        scratch_shapes=[
            pltpu.VMEM((SLOTS, TOK, WIDTH), BF16),
            pltpu.VMEM((SLOTS, TOK, WIDTH), BF16),
            pltpu.VMEM((RANKS, TAIL, DIM), F32),
            pltpu.VMEM((REQ, HEADS, 32, DIM), F32),
            pltpu.VMEM((SLOTS, rows, DIM), F32),
            pltpu.VMEM((SLOTS, rows, DIM), F32),
            pltpu.VMEM((REQ, rows, DIM), F32),
            pltpu.VMEM((REQ, rows, DIM), F32),
            pltpu.VMEM((REQ, rows, DIM), F32),
            pltpu.VMEM((REQ, STEPS, TAIL, DIM), F32),
            DMA((2, SLOTS)),
        ],
        compiler_params=pltpu.CompilerParams(vmem_limit_bytes=50 << 20),
        cost_estimate=pl.CostEstimate(flops=2 ** 29, bytes_accessed=2 ** 23, transcendentals=2 ** 18),
        name="attend",
    )(plan, spread, blocks)
    landed = lax.all_to_all(sent, "blk", split_axis=0, concat_axis=0, tiled=True)

    return pl.pallas_call(
        place_kernel,
        out_shape=(jax.ShapeDtypeStruct(queries.shape, BF16), pool, pool),
        in_specs=[SMEM, VMEM, HBM, HBM],
        out_specs=(VMEM, HBM, HBM),
        scratch_shapes=[pltpu.VMEM((RANKS, TAIL, DIM), F32), DMA],
        input_output_aliases={2: 1, 3: 2},
        compiler_params=pltpu.CompilerParams(vmem_limit_bytes=16 << 20),
        name="place",
    )(plan, landed, keys, values)


def solution(mesh):
    both = ("grp", "blk")
    return jax.shard_map(
        per_device,
        mesh=mesh,
        in_specs=(P(both, None), *[P(both, None, None)] * 4, P("grp"), P("grp", None), P("grp")),
        out_specs=(P(both, None), P(both, None, None), P(both, None, None)),
        check_vma=False,
    )
```

```python
import jax
import jax.numpy as jnp
from jax import lax
from jax.experimental import pallas as pl
from jax.experimental.pallas import tpu as pltpu
from jax.sharding import PartitionSpec as P

RANKS = 16
SLOTS = 8
KEPT = 6
SPILL = 32
REQ = 4
STEPS = 4
COLS = 32
TOK = 128
HEADS = 8
GROUP = 5
DIM = 128
WIDTH = HEADS * DIM
HALF = 64
DATA = 256
TAIL = 48
LENGTHS = 32
TABLE = 64
REQUEST = 32
BOUND = 40
HOME = 48
PLAN = 128
FAR = 1 << 22
NEG = -1e30
ANY = pl.BlockSpec(memory_space=pl.ANY)
SMEM = pl.BlockSpec(memory_space=pltpu.SMEM)
VMEM = pl.BlockSpec(memory_space=pltpu.VMEM)
HBM = pl.BlockSpec(memory_space=pltpu.HBM)
DMA = pltpu.SemaphoreType.DMA
F32 = jnp.float32
BF16 = jnp.bfloat16


def pack_kernel(q, pk, pv, out, q_in, q_rows, buf, stage, q_sem, sem, out_sem):
    loads, stores = [], []
    for b in range(2):
        for kv, source in enumerate((pk, pv)):
            for half in range(2):
                n = b * 4 + kv * 2 + half
                loads.append(pltpu.make_async_copy(source.at[b, pl.ds(half * HALF, HALF)], buf.at[n], sem.at[n]))
                loads[-1].start()
    get = pltpu.make_async_copy(q, q_in, q_sem)
    get.start()
    for n in range(4):
        part = pl.ds(n * HALF, HALF)
        stores.append(pltpu.make_async_copy(stage.at[:, part], out.at[:, part], out_sem.at[n]))
    part = pl.ds(DATA, TAIL)
    stores.append(pltpu.make_async_copy(stage.at[:, part], out.at[:, part], out_sem.at[4]))
    q_rows[...] = jnp.zeros_like(q_rows)
    for n, load in enumerate(loads):
        load.wait()
        at = (n >> 1) * HALF
        for h in range(HEADS):
            stage[2 * h + (n & 1), at : at + HALF, :] = buf[n, :, h * DIM : (h + 1) * DIM]
        if n % 2 == 1:
            stores[n >> 1].start()
        if n == 3:
            get.wait()
            for m in range(HEADS * GROUP):
                q_rows[m : m + 1, :] = q_in[:, m * DIM : (m + 1) * DIM].astype(F32)
            q_bf = q_rows[...].astype(BF16)
            for k in range(RANKS):
                stage[k, DATA:, :] = q_bf
            stores[4].start()
    for c in stores:
        c.wait()


def load_kernel(
    ints, ck, cv, pk, pv, out_k, out_v, reads_out, plan, far,
    inverse, taken, slot_of, count, buf, in_sem, out_sem, get_sem, far_sem,
):
    me = lax.axis_index("blk")
    reads, writes = [], []
    for i in range(2):
        for kv, source in enumerate((pk, pv)):
            e = KEPT + i
            reads.append(pltpu.make_async_copy(source.at[i], buf.at[kv, e], in_sem.at[kv, e]))
            writes.append([pltpu.make_async_copy(buf.at[kv, e], reads_out.at[kv, e], get_sem.at[kv, e])])
            reads[-1].start()
    for s in range(SLOTS):
        taken[s] = 0
    for k in range(RANKS):
        count[k] = 0
    for k in range(PLAN):
        plan[k] = 0

    def mark(b, _):
        slot = ints[b]
        t = slot >> 3
        n = count[t]
        count[t] = n + 1
        plan[b] = t * 2 + n

        @pl.when(t == me)
        def _():
            taken[slot & 7] = 1
            plan[HOME + n] = slot & 7

        return 0

    lax.fori_loop(0, SPILL, mark, 0)

    def pick(s, n):
        @pl.when(taken[s] == 0)
        def _():
            slot_of[n] = s

        return n + 1 - taken[s]

    lax.fori_loop(0, SLOTS, pick, 0)
    for e in range(KEPT):
        s = slot_of[e]
        for kv, (source, out) in enumerate(((ck, out_k), (cv, out_v))):
            reads.append(pltpu.make_async_copy(source.at[s], buf.at[kv, e], in_sem.at[kv, e]))
            writes.append([
                pltpu.make_async_copy(buf.at[kv, e], reads_out.at[kv, e], get_sem.at[kv, e]),
                pltpu.make_async_copy(buf.at[kv, e], out.at[s], out_sem.at[kv, e]),
            ])
            reads[-1].start()

    def invert(i, _):
        for r in range(REQ):
            inverse[ints[TABLE + r * COLS + i]] = r * COLS + i
        return 0

    lax.fori_loop(0, COLS, invert, 0)
    for e in range(SLOTS):
        place = inverse[me * SLOTS + slot_of[e] if e < KEPT else ints[me * 2 + (e - KEPT)]]
        plan[REQUEST + e] = place >> 5
        plan[BOUND + e] = ints[LENGTHS + (place >> 5)] - (place & 31) * TOK - (STEPS - 1)
    copy = pltpu.make_async_copy(plan, far.at[pl.ds(0, PLAN)], far_sem)
    copy.start()
    for r, w in zip(reads, writes):
        r.wait()
        for c in w:
            c.start()
    for w in writes:
        for c in w:
            c.wait()
    copy.wait()


def attend_kernel(
    far, spread, blocks, sent, plan, kbuf, vbuf, q_rows, q_s, s_buf, top_s, m_s, l_s, o_s, row_s, sem, plan_sem
):
    copy = pltpu.make_async_copy(far.at[pl.ds(0, PLAN)], plan, plan_sem)
    copy.start()
    order = tuple(range(SLOTS))
    loads = {}
    for e in order:
        for kv, buf in enumerate((kbuf, vbuf)):
            loads[e, kv] = pltpu.make_async_copy(blocks.at[kv, e], buf.at[e], sem.at[kv, e])
    for kv in range(2):
        for e in order:
            loads[e, kv].start()
    m_s[...] = jnp.full_like(m_s, NEG)
    l_s[...] = jnp.zeros_like(l_s)
    o_s[...] = jnp.zeros_like(o_s)
    q_s[...] = jnp.zeros_like(q_s)
    for i in range(RANKS):
        a, r = i // REQ, i % REQ
        q_rows[i] = spread[i, DATA:, :].astype(F32)
        for h in range(HEADS):
            q_s[r, h, a * 8 : a * 8 + GROUP, :] = q_rows[i, h * GROUP : (h + 1) * GROUP, :]
    copy.wait()
    request = [plan[REQUEST + e] for e in range(SLOTS)]
    bound = [plan[BOUND + e] for e in range(SLOTS)]
    rows = HEADS * 32
    step = (lax.broadcasted_iota(jnp.int32, (rows, TOK), 0) & 31) >> 3
    token = lax.broadcasted_iota(jnp.int32, (rows, TOK), 1) - step
    for n, e in enumerate(order):
        if n % 2 == 0:
            loads[order[n], 0].wait()
            loads[order[n + 1], 0].wait()
        s = jnp.concatenate(
            [
                lax.dot_general(
                    q_s[request[e], h].astype(BF16), kbuf[e, :, h * DIM : (h + 1) * DIM],
                    (((1,), (1,)), ((), ())), preferred_element_type=F32,
                )
                for h in range(HEADS)
            ],
            axis=0,
        ) * (DIM ** -0.5)
        s = jnp.where(token < bound[e], s, NEG)
        s_buf[e] = s
        top_s[e] = jnp.broadcast_to(jnp.max(s, axis=1, keepdims=True), (rows, TOK))
    for b in range(SPILL):
        to = plan[b]
        sent[to >> 1, pl.ds(pl.multiple_of((to & 1) * 128, 128), 128), :] = spread[
            b >> 1, (b & 1) * 128 : (b & 1) * 128 + 128, :
        ]
    for e in range(SLOTS):
        m_s[request[e]] = jnp.maximum(m_s[request[e]], top_s[e])
    for n, e in enumerate(order):
        if n % 4 == 0:
            for other in order[n : n + 4]:
                loads[other, 1].wait()
        w = jnp.where(token < bound[e], jnp.exp(s_buf[e] - m_s[request[e]]), 0.0)
        p = w.astype(BF16)
        o = jnp.concatenate(
            [
                jnp.dot(
                    p[h * 32 : (h + 1) * 32], vbuf[e, :, h * DIM : (h + 1) * DIM],
                    preferred_element_type=F32,
                )
                for h in range(HEADS)
            ],
            axis=0,
        )
        top_s[e] = jnp.broadcast_to(jnp.sum(w, axis=1, keepdims=True), (rows, TOK))
        s_buf[e] = o
    for e in range(SLOTS):
        l_s[request[e]] = l_s[request[e]] + top_s[e]
        o_s[request[e]] = o_s[request[e]] + s_buf[e]

    sub = lax.broadcasted_iota(jnp.int32, (8, DIM), 0)
    lane = lax.broadcasted_iota(jnp.int32, (8, DIM), 1)
    for r in range(REQ):
        for a in range(STEPS):
            for h in range(HEADS):
                at = h * 32 + a * 8
                row_s[r, a, h * GROUP : (h + 1) * GROUP, :] = o_s[r, at : at + GROUP, :]
                ml = jnp.where(lane == sub, m_s[r, at : at + 8, :], 0.0)
                ml = jnp.where(lane == sub + 8, l_s[r, at : at + 8, :], ml)
                row_s[r, a, 40 + h : 41 + h, :] = jnp.sum(ml, axis=0, keepdims=True)
            ml = row_s[r, a, 40:, :]
            hi = ml.astype(BF16).astype(F32)
            mid = (ml - hi).astype(BF16).astype(F32)
            row_s[r, a, 40:, :] = hi + pltpu.roll(mid, 16, 1) + pltpu.roll(ml - hi - mid, 32, 1)
            sent[a * REQ + r, DATA:, :] = row_s[r, a].astype(BF16)


def place_kernel(plan, z, key_in, value_in, att, out_k, out_v, tail, sem):
    for n in range(2):
        slot = plan[HOME + n]
        for c in range(RANKS):
            for kv, out in enumerate((out_k, out_v)):
                pltpu.make_async_copy(
                    z.at[c, pl.ds(n * 128 + kv * HALF, HALF)],
                    out.at[slot, pl.ds((c % 2) * HALF, HALF), pl.ds((c // 2) * DIM, DIM)],
                    sem,
                ).start()
    for k in range(RANKS):
        tail[k] = z[k, DATA:, :].astype(F32)
    sub = lax.broadcasted_iota(jnp.int32, (8, DIM), 0)
    lane = lax.broadcasted_iota(jnp.int32, (8, DIM), 1)
    state = []
    for k in range(RANKS):
        ml = tail[k, 40:, :]
        state.append(ml + (pltpu.roll(ml, DIM - 16, 1) + pltpu.roll(ml, DIM - 32, 1)))
    top = state[0]
    for x in state[1:]:
        top = jnp.maximum(top, x)
    scales = [jnp.exp(x - top) for x in state]
    down = jnp.zeros((8, DIM), F32)
    for x, scale in zip(state, scales):
        down = down + scale * pltpu.roll(x, DIM - 8, 1)
    inverse = jnp.where(lane < GROUP, 1.0 / jnp.where(lane < GROUP, down, 1.0), 0.0)
    scales = [jnp.where(lane < GROUP, scale, 0.0) * inverse for scale in scales]
    for h in range(HEADS):
        acc = jnp.zeros((GROUP, DIM), F32)
        for k in range(RANKS):
            col = jnp.sum(jnp.where(lane == sub, scales[k][h : h + 1], 0.0), axis=1, keepdims=True)
            acc = acc + col[:GROUP] * tail[k, h * GROUP : (h + 1) * GROUP, :]
        for g in range(GROUP):
            n = h * GROUP + g
            att[:, n * DIM : (n + 1) * DIM] = acc[g : g + 1].astype(BF16)
    pltpu.make_async_copy(z.at[:, pl.ds(0, DATA)], z.at[:, pl.ds(0, DATA)], sem).wait()


def per_device(queries, cache_keys, values_prior, prefill_keys, prefill_values, lengths, table, spill):
    pool = jax.ShapeDtypeStruct(cache_keys.shape, BF16)
    message = jax.ShapeDtypeStruct((RANKS, DATA + TAIL, DIM), BF16)
    rows = HEADS * 32
    ints = jnp.concatenate([spill, lengths, jnp.zeros((TABLE - LENGTHS - REQ,), jnp.int32), table.reshape(-1)])
    packed = pl.pallas_call(
        pack_kernel,
        out_shape=message,
        in_specs=[HBM] * 3,
        out_specs=HBM,
        scratch_shapes=[
            pltpu.VMEM(queries.shape, BF16),
            pltpu.VMEM((TAIL, DIM), F32),
            pltpu.VMEM((8, HALF, WIDTH), BF16),
            pltpu.VMEM(message.shape, BF16),
            DMA,
            DMA((8,)),
            DMA((5,)),
        ],
        compiler_params=pltpu.CompilerParams(vmem_limit_bytes=59 << 20),
        name="pack",
    )(queries, prefill_keys, prefill_values)
    spread = lax.all_to_all(packed, "blk", split_axis=0, concat_axis=0, tiled=True)

    keys, values, blocks, plan, far = pl.pallas_call(
        load_kernel,
        out_shape=(
            pool,
            pool,
            jax.ShapeDtypeStruct((2, SLOTS, TOK, WIDTH), BF16),
            jax.ShapeDtypeStruct((PLAN,), jnp.int32),
            jax.ShapeDtypeStruct((FAR,), jnp.int32),
        ),
        in_specs=[SMEM] + [HBM] * 4,
        out_specs=(HBM, HBM, HBM, SMEM, HBM),
        scratch_shapes=[
            pltpu.SMEM((RANKS * SLOTS,), jnp.int32),
            pltpu.SMEM((SLOTS,), jnp.int32),
            pltpu.SMEM((SLOTS,), jnp.int32),
            pltpu.SMEM((RANKS,), jnp.int32),
            pltpu.VMEM((2, SLOTS, TOK, WIDTH), BF16),
            DMA((2, SLOTS)),
            DMA((2, SLOTS)),
            DMA((2, SLOTS)),
            DMA,
        ],
        compiler_params=pltpu.CompilerParams(vmem_limit_bytes=58 << 20),
        cost_estimate=pl.CostEstimate(flops=0, bytes_accessed=7 << 20, transcendentals=0),
        name="load",
    )(ints, cache_keys, values_prior, prefill_keys, prefill_values)

    sent = pl.pallas_call(
        attend_kernel,
        out_shape=message,
        in_specs=[HBM, VMEM, HBM],
        out_specs=VMEM,
        scratch_shapes=[
            pltpu.SMEM((PLAN,), jnp.int32),
            pltpu.VMEM((SLOTS, TOK, WIDTH), BF16),
            pltpu.VMEM((SLOTS, TOK, WIDTH), BF16),
            pltpu.VMEM((RANKS, TAIL, DIM), F32),
            pltpu.VMEM((REQ, HEADS, 32, DIM), F32),
            pltpu.VMEM((SLOTS, rows, DIM), F32),
            pltpu.VMEM((SLOTS, rows, DIM), F32),
            pltpu.VMEM((REQ, rows, DIM), F32),
            pltpu.VMEM((REQ, rows, DIM), F32),
            pltpu.VMEM((REQ, rows, DIM), F32),
            pltpu.VMEM((REQ, STEPS, TAIL, DIM), F32),
            DMA((2, SLOTS)),
            DMA,
        ],
        compiler_params=pltpu.CompilerParams(vmem_limit_bytes=50 << 20),
        cost_estimate=pl.CostEstimate(flops=2 ** 29, bytes_accessed=2 ** 23, transcendentals=2 ** 18),
        name="attend",
    )(far, spread, blocks)
    landed = lax.all_to_all(sent, "blk", split_axis=0, concat_axis=0, tiled=True)

    return pl.pallas_call(
        place_kernel,
        out_shape=(jax.ShapeDtypeStruct(queries.shape, BF16), pool, pool),
        in_specs=[SMEM, VMEM, HBM, HBM],
        out_specs=(VMEM, HBM, HBM),
        scratch_shapes=[pltpu.VMEM((RANKS, TAIL, DIM), F32), DMA],
        input_output_aliases={2: 1, 3: 2},
        compiler_params=pltpu.CompilerParams(vmem_limit_bytes=16 << 20),
        name="place",
    )(plan, landed, keys, values)


def solution(mesh):
    both = ("grp", "blk")
    return jax.shard_map(
        per_device,
        mesh=mesh,
        in_specs=(P(both, None), *[P(both, None, None)] * 4, P("grp"), P("grp", None), P("grp")),
        out_specs=(P(both, None), P(both, None, None), P(both, None, None)),
        check_vma=False,
    )
```

```python
import jax
import jax.numpy as jnp
from jax import lax
from jax.experimental import pallas as pl
from jax.experimental.pallas import tpu as pltpu
from jax.sharding import PartitionSpec as P

RANKS = 16
SLOTS = 8
KEPT = 6
SPILL = 32
REQ = 4
STEPS = 4
COLS = 32
TOK = 128
HEADS = 8
GROUP = 5
DIM = 128
WIDTH = HEADS * DIM
HALF = 64
DATA = 256
TAIL = 48
LENGTHS = 32
TABLE = 64
REQUEST = 32
BOUND = 40
HOME = 48
PLAN = 128
FAR = 1 << 22
NEG = -1e30
ANY = pl.BlockSpec(memory_space=pl.ANY)
SMEM = pl.BlockSpec(memory_space=pltpu.SMEM)
VMEM = pl.BlockSpec(memory_space=pltpu.VMEM)
HBM = pl.BlockSpec(memory_space=pltpu.HBM)
DMA = pltpu.SemaphoreType.DMA
F32 = jnp.float32
BF16 = jnp.bfloat16


def pack_kernel(q, pk, pv, out, q_in, q_rows, buf, stage, q_sem, sem, out_sem):
    loads, stores = [], []
    for b in range(2):
        for kv, source in enumerate((pk, pv)):
            for half in range(2):
                n = b * 4 + kv * 2 + half
                loads.append(pltpu.make_async_copy(source.at[b, pl.ds(half * HALF, HALF)], buf.at[n], sem.at[n]))
                loads[-1].start()
    get = pltpu.make_async_copy(q, q_in, q_sem)
    get.start()
    for n in range(4):
        part = pl.ds(n * HALF, HALF)
        stores.append(pltpu.make_async_copy(stage.at[:, part], out.at[:, part], out_sem.at[n]))
    part = pl.ds(DATA, TAIL)
    stores.append(pltpu.make_async_copy(stage.at[:, part], out.at[:, part], out_sem.at[4]))
    q_rows[...] = jnp.zeros_like(q_rows)
    for n, load in enumerate(loads):
        load.wait()
        at = (n >> 1) * HALF
        for h in range(HEADS):
            stage[2 * h + (n & 1), at : at + HALF, :] = buf[n, :, h * DIM : (h + 1) * DIM]
        if n % 2 == 1:
            stores[n >> 1].start()
        if n == 3:
            get.wait()
            for m in range(HEADS * GROUP):
                q_rows[m : m + 1, :] = q_in[:, m * DIM : (m + 1) * DIM].astype(F32)
            q_bf = q_rows[...].astype(BF16)
            for k in range(RANKS):
                stage[k, DATA:, :] = q_bf
            stores[4].start()
    for c in stores:
        c.wait()


def load_kernel(
    ints, ck, cv, pk, pv, out_k, out_v, reads_out, plan, far,
    inverse, taken, slot_of, count, buf, in_sem, out_sem, get_sem, far_sem,
):
    me = lax.axis_index("blk")
    reads, writes = [], []
    for i in range(2):
        for kv, source in enumerate((pk, pv)):
            e = KEPT + i
            reads.append(pltpu.make_async_copy(source.at[i], buf.at[kv, e], in_sem.at[kv, e]))
            writes.append([pltpu.make_async_copy(buf.at[kv, e], reads_out.at[kv, e], get_sem.at[kv, e])])
            reads[-1].start()
    for s in range(SLOTS):
        taken[s] = 0
    for k in range(RANKS):
        count[k] = 0
    for k in range(PLAN):
        plan[k] = 0

    def mark(b, _):
        slot = ints[b]
        t = slot >> 3
        n = count[t]
        count[t] = n + 1
        plan[b] = t * 2 + n

        @pl.when(t == me)
        def _():
            taken[slot & 7] = 1
            plan[HOME + n] = slot & 7

        return 0

    lax.fori_loop(0, SPILL, mark, 0)

    def pick(s, n):
        @pl.when(taken[s] == 0)
        def _():
            slot_of[n] = s

        return n + 1 - taken[s]

    lax.fori_loop(0, SLOTS, pick, 0)
    for e in range(KEPT):
        s = slot_of[e]
        for kv, (source, out) in enumerate(((ck, out_k), (cv, out_v))):
            reads.append(pltpu.make_async_copy(source.at[s], buf.at[kv, e], in_sem.at[kv, e]))
            writes.append([
                pltpu.make_async_copy(buf.at[kv, e], reads_out.at[kv, e], get_sem.at[kv, e]),
                pltpu.make_async_copy(buf.at[kv, e], out.at[s], out_sem.at[kv, e]),
            ])
            reads[-1].start()

    def invert(i, _):
        for r in range(REQ):
            inverse[ints[TABLE + r * COLS + i]] = r * COLS + i
        return 0

    lax.fori_loop(0, COLS, invert, 0)
    for e in range(SLOTS):
        place = inverse[me * SLOTS + slot_of[e] if e < KEPT else ints[me * 2 + (e - KEPT)]]
        plan[REQUEST + e] = place >> 5
        plan[BOUND + e] = ints[LENGTHS + (place >> 5)] - (place & 31) * TOK - (STEPS - 1)
    copy = pltpu.make_async_copy(plan, far.at[pl.ds(0, PLAN)], far_sem)
    copy.start()
    for r, w in zip(reads, writes):
        r.wait()
        for c in w:
            c.start()
    for w in writes:
        for c in w:
            c.wait()
    copy.wait()


def attend_kernel(
    far, spread, blocks, sent, plan, kbuf, vbuf, q_rows, q_s, s_buf, top_s, m_s, l_s, o_s, row_s, p_s, sem, plan_sem
):
    copy = pltpu.make_async_copy(far.at[pl.ds(0, PLAN)], plan, plan_sem)
    copy.start()
    order = tuple(range(SLOTS))
    loads = {}
    for e in order:
        for kv, buf in enumerate((kbuf, vbuf)):
            loads[e, kv] = pltpu.make_async_copy(blocks.at[kv, e], buf.at[e], sem.at[kv, e])
    for kv in range(2):
        for e in order:
            loads[e, kv].start()
    m_s[...] = jnp.full_like(m_s, NEG)
    l_s[...] = jnp.zeros_like(l_s)
    o_s[...] = jnp.zeros_like(o_s)
    q_s[...] = jnp.zeros_like(q_s)
    for i in range(RANKS):
        a, r = i // REQ, i % REQ
        q_rows[i] = spread[i, DATA:, :].astype(F32)
        for h in range(HEADS):
            q_s[r, h, a * 8 : a * 8 + GROUP, :] = q_rows[i, h * GROUP : (h + 1) * GROUP, :]
    copy.wait()
    request = [plan[REQUEST + e] for e in range(SLOTS)]
    bound = [plan[BOUND + e] for e in range(SLOTS)]
    rows = HEADS * 32
    step = (lax.broadcasted_iota(jnp.int32, (rows, TOK), 0) & 31) >> 3
    token = lax.broadcasted_iota(jnp.int32, (rows, TOK), 1) - step
    for n, e in enumerate(order):
        if n % 2 == 0:
            loads[order[n], 0].wait()
            loads[order[n + 1], 0].wait()
        s = jnp.concatenate(
            [
                lax.dot_general(
                    q_s[request[e], h].astype(BF16), kbuf[e, :, h * DIM : (h + 1) * DIM],
                    (((1,), (1,)), ((), ())), preferred_element_type=F32,
                )
                for h in range(HEADS)
            ],
            axis=0,
        ) * (DIM ** -0.5)
        s = jnp.where(token < bound[e], s, NEG)
        s_buf[e] = s
        top_s[e] = jnp.broadcast_to(jnp.max(s, axis=1, keepdims=True), (rows, TOK))
    for b in range(SPILL):
        to = plan[b]
        sent[to >> 1, pl.ds(pl.multiple_of((to & 1) * 128, 128), 128), :] = spread[
            b >> 1, (b & 1) * 128 : (b & 1) * 128 + 128, :
        ]
    for e in range(SLOTS):
        m_s[request[e]] = jnp.maximum(m_s[request[e]], top_s[e])
    for e in order:
        w = jnp.where(token < bound[e], jnp.exp(s_buf[e] - m_s[request[e]]), 0.0)
        p_s[e] = w.astype(BF16)
        top_s[e] = jnp.broadcast_to(jnp.sum(w, axis=1, keepdims=True), (rows, TOK))
    for e in order:
        l_s[request[e]] = l_s[request[e]] + top_s[e]
    for n, e in enumerate(order):
        if n % 4 == 0:
            for other in order[n : n + 4]:
                loads[other, 1].wait()
        p = p_s[e]
        o = jnp.concatenate(
            [
                jnp.dot(
                    p[h * 32 : (h + 1) * 32], vbuf[e, :, h * DIM : (h + 1) * DIM],
                    preferred_element_type=F32,
                )
                for h in range(HEADS)
            ],
            axis=0,
        )
        s_buf[e] = o
    for e in range(SLOTS):
        o_s[request[e]] = o_s[request[e]] + s_buf[e]

    sub = lax.broadcasted_iota(jnp.int32, (8, DIM), 0)
    lane = lax.broadcasted_iota(jnp.int32, (8, DIM), 1)
    for r in range(REQ):
        for a in range(STEPS):
            for h in range(HEADS):
                at = h * 32 + a * 8
                row_s[r, a, h * GROUP : (h + 1) * GROUP, :] = o_s[r, at : at + GROUP, :]
                ml = jnp.where(lane == sub, m_s[r, at : at + 8, :], 0.0)
                ml = jnp.where(lane == sub + 8, l_s[r, at : at + 8, :], ml)
                row_s[r, a, 40 + h : 41 + h, :] = jnp.sum(ml, axis=0, keepdims=True)
            ml = row_s[r, a, 40:, :]
            hi = ml.astype(BF16).astype(F32)
            mid = (ml - hi).astype(BF16).astype(F32)
            row_s[r, a, 40:, :] = hi + pltpu.roll(mid, 16, 1) + pltpu.roll(ml - hi - mid, 32, 1)
            sent[a * REQ + r, DATA:, :] = row_s[r, a].astype(BF16)


def place_kernel(plan, z, key_in, value_in, att, out_k, out_v, tail, sem):
    for n in range(2):
        slot = plan[HOME + n]
        for c in range(RANKS):
            for kv, out in enumerate((out_k, out_v)):
                pltpu.make_async_copy(
                    z.at[c, pl.ds(n * 128 + kv * HALF, HALF)],
                    out.at[slot, pl.ds((c % 2) * HALF, HALF), pl.ds((c // 2) * DIM, DIM)],
                    sem,
                ).start()
    for k in range(RANKS):
        tail[k] = z[k, DATA:, :].astype(F32)
    sub = lax.broadcasted_iota(jnp.int32, (8, DIM), 0)
    lane = lax.broadcasted_iota(jnp.int32, (8, DIM), 1)
    state = []
    for k in range(RANKS):
        ml = tail[k, 40:, :]
        state.append(ml + (pltpu.roll(ml, DIM - 16, 1) + pltpu.roll(ml, DIM - 32, 1)))
    top = state[0]
    for x in state[1:]:
        top = jnp.maximum(top, x)
    scales = [jnp.exp(x - top) for x in state]
    down = jnp.zeros((8, DIM), F32)
    for x, scale in zip(state, scales):
        down = down + scale * pltpu.roll(x, DIM - 8, 1)
    inverse = jnp.where(lane < GROUP, 1.0 / jnp.where(lane < GROUP, down, 1.0), 0.0)
    scales = [jnp.where(lane < GROUP, scale, 0.0) * inverse for scale in scales]
    for h in range(HEADS):
        acc = jnp.zeros((GROUP, DIM), F32)
        for k in range(RANKS):
            col = jnp.sum(jnp.where(lane == sub, scales[k][h : h + 1], 0.0), axis=1, keepdims=True)
            acc = acc + col[:GROUP] * tail[k, h * GROUP : (h + 1) * GROUP, :]
        for g in range(GROUP):
            n = h * GROUP + g
            att[:, n * DIM : (n + 1) * DIM] = acc[g : g + 1].astype(BF16)
    pltpu.make_async_copy(z.at[:, pl.ds(0, DATA)], z.at[:, pl.ds(0, DATA)], sem).wait()


def per_device(queries, cache_keys, values_prior, prefill_keys, prefill_values, lengths, table, spill):
    pool = jax.ShapeDtypeStruct(cache_keys.shape, BF16)
    message = jax.ShapeDtypeStruct((RANKS, DATA + TAIL, DIM), BF16)
    rows = HEADS * 32
    ints = jnp.concatenate([spill, lengths, jnp.zeros((TABLE - LENGTHS - REQ,), jnp.int32), table.reshape(-1)])
    packed = pl.pallas_call(
        pack_kernel,
        out_shape=message,
        in_specs=[HBM] * 3,
        out_specs=HBM,
        scratch_shapes=[
            pltpu.VMEM(queries.shape, BF16),
            pltpu.VMEM((TAIL, DIM), F32),
            pltpu.VMEM((8, HALF, WIDTH), BF16),
            pltpu.VMEM(message.shape, BF16),
            DMA,
            DMA((8,)),
            DMA((5,)),
        ],
        compiler_params=pltpu.CompilerParams(vmem_limit_bytes=59 << 20),
        name="pack",
    )(queries, prefill_keys, prefill_values)
    spread = lax.all_to_all(packed, "blk", split_axis=0, concat_axis=0, tiled=True)

    keys, values, blocks, plan, far = pl.pallas_call(
        load_kernel,
        out_shape=(
            pool,
            pool,
            jax.ShapeDtypeStruct((2, SLOTS, TOK, WIDTH), BF16),
            jax.ShapeDtypeStruct((PLAN,), jnp.int32),
            jax.ShapeDtypeStruct((FAR,), jnp.int32),
        ),
        in_specs=[SMEM] + [HBM] * 4,
        out_specs=(HBM, HBM, HBM, SMEM, HBM),
        scratch_shapes=[
            pltpu.SMEM((RANKS * SLOTS,), jnp.int32),
            pltpu.SMEM((SLOTS,), jnp.int32),
            pltpu.SMEM((SLOTS,), jnp.int32),
            pltpu.SMEM((RANKS,), jnp.int32),
            pltpu.VMEM((2, SLOTS, TOK, WIDTH), BF16),
            DMA((2, SLOTS)),
            DMA((2, SLOTS)),
            DMA((2, SLOTS)),
            DMA,
        ],
        compiler_params=pltpu.CompilerParams(vmem_limit_bytes=58 << 20),
        cost_estimate=pl.CostEstimate(flops=0, bytes_accessed=7 << 20, transcendentals=0),
        name="load",
    )(ints, cache_keys, values_prior, prefill_keys, prefill_values)

    sent = pl.pallas_call(
        attend_kernel,
        out_shape=message,
        in_specs=[HBM, VMEM, HBM],
        out_specs=VMEM,
        scratch_shapes=[
            pltpu.SMEM((PLAN,), jnp.int32),
            pltpu.VMEM((SLOTS, TOK, WIDTH), BF16),
            pltpu.VMEM((SLOTS, TOK, WIDTH), BF16),
            pltpu.VMEM((RANKS, TAIL, DIM), F32),
            pltpu.VMEM((REQ, HEADS, 32, DIM), F32),
            pltpu.VMEM((SLOTS, rows, DIM), F32),
            pltpu.VMEM((SLOTS, rows, DIM), F32),
            pltpu.VMEM((REQ, rows, DIM), F32),
            pltpu.VMEM((REQ, rows, DIM), F32),
            pltpu.VMEM((REQ, rows, DIM), F32),
            pltpu.VMEM((REQ, STEPS, TAIL, DIM), F32),
            pltpu.VMEM((SLOTS, rows, TOK), BF16),
            DMA((2, SLOTS)),
            DMA,
        ],
        compiler_params=pltpu.CompilerParams(vmem_limit_bytes=50 << 20),
        cost_estimate=pl.CostEstimate(flops=2 ** 29, bytes_accessed=2 ** 23, transcendentals=2 ** 18),
        name="attend",
    )(far, spread, blocks)
    landed = lax.all_to_all(sent, "blk", split_axis=0, concat_axis=0, tiled=True)

    return pl.pallas_call(
        place_kernel,
        out_shape=(jax.ShapeDtypeStruct(queries.shape, BF16), pool, pool),
        in_specs=[SMEM, VMEM, HBM, HBM],
        out_specs=(VMEM, HBM, HBM),
        scratch_shapes=[pltpu.VMEM((RANKS, TAIL, DIM), F32), DMA],
        input_output_aliases={2: 1, 3: 2},
        compiler_params=pltpu.CompilerParams(vmem_limit_bytes=16 << 20),
        name="place",
    )(plan, landed, keys, values)


def solution(mesh):
    both = ("grp", "blk")
    return jax.shard_map(
        per_device,
        mesh=mesh,
        in_specs=(P(both, None), *[P(both, None, None)] * 4, P("grp"), P("grp", None), P("grp")),
        out_specs=(P(both, None), P(both, None, None), P(both, None, None)),
        check_vma=False,
    )
```
